128 devices in a mesh: dp: 16 (over z_lo, y, core), seq: 8 (over z_hi, x).
Axes of the slice: x: 4, y: 4, z: 4 (z_hi: 2, z_lo: 2; z = z_hi * 2 + z_lo), core: 2. Of those that a mesh axis runs over, the one named last changes fastest.
Arguments:
- sequence_features: bfloat16 [16, 6144, 1024], P('dp', 'seq'), may hold values from -6 to 6
- conv_weight: bfloat16 [1024, 5760], P('dp'), may hold values from -0.078125 to 0.078125
- output_grad: bfloat16 [16, 3072, 1152], P('dp', 'seq'), may hold values from -6 to 6
Outputs:
- pooled: float32 [16, 3072, 1152], P('dp', 'seq')
- feature_grad: float32 [16, 6144, 1024], P('dp', 'seq')
- weight_grad: float32 [1024, 5760], P('dp')
The draws below stay inside these ranges and needn't reach their ends.
All inputs are finite; a program needn't handle non-finite values.
Results may differ from the reference program's by a relative error of at most 0.0029.
Values may be sent and summed in bfloat16 or wider, within the bound.
No kernel may reach another device: no remote copies, remote signals or barrier semaphores. Data moves between devices by JAX's collectives and lax.ppermute only.
A program may use at most 256 MiB of HBM per device.

```python
import jax
import jax.numpy as jnp
from jax import lax

CIN = 1024
COUT = 1152
KW = 5
EXAMPLES = 16
LENGTH = 6144


def with_spikes(result, rng, source, target, shards_of, factor):
    owner, partner = [(jnp.arange(result.shape[position]) // (result.shape[position] // shards_of)).reshape([-1 if axis == position else 1 for axis in range(result.ndim)]) for position in (source, target)]
    chosen = jax.random.permutation(rng, shards_of)[partner]
    strong = (owner == chosen) | (owner == (partner + shards_of // 2) % shards_of)
    return jnp.where(strong, factor * result, result)


def block_levels(stream_key, extent, pieces, least, high):
    def one(position, shards_of):
        draws = jax.random.uniform(jax.random.fold_in(jax.random.fold_in(stream_key, 6), position), (shards_of,), jnp.float32, least / len(pieces), high / len(pieces))
        return jnp.repeat(jnp.exp(draws), extent[position] // shards_of).reshape((-1,) + (1,) * (len(extent) - position - 1))

    factor_of = one(*pieces[0])
    for cut in pieces[1:]:
        factor_of = factor_of * one(*cut)
    return factor_of


def gaussian(stream_key, dims, width, reach, split=(), dtype=jnp.bfloat16):
    values = jax.random.normal(stream_key, dims, jnp.float32) * width
    if len(split) > 0:
        values = block_levels(stream_key, dims, split, -0.22, 0.18) * values
    return jnp.clip(values, min=-reach, max=reach).astype(dtype)


def gaussian_with(stream_key, dims, spread, bound, pieces, heavy, dtype=jnp.bfloat16):
    entries = spread * jax.random.normal(stream_key, dims, jnp.float32)
    if pieces:
        entries = entries * block_levels(stream_key, dims, pieces, -0.22, 0.18)
    return jnp.clip(with_spikes(entries, jax.random.fold_in(stream_key, 3), *heavy), -bound, bound).astype(dtype)


def setup_inputs(seed: int = 0) -> dict:
    keys = jax.random.split(jax.random.key(seed), 4)
    return {
        "sequence_features": gaussian_with(keys[0], (EXAMPLES, LENGTH, CIN), 1.0, 6.0, ((0, 16), (1, 8)), (0, 2, 16, 2.0)),
        "conv_weight": gaussian(keys[1], (CIN, KW * COUT), (KW * CIN) ** -0.5, 0.078125, ((0, 16),)),
        "output_grad": gaussian(keys[2], (EXAMPLES, LENGTH // 2, COUT), 1.0, 6.0, ((0, 16), (1, 8))),
    }


def exact_gelu(value):
    return jax.nn.gelu(value, approximate=False)

def reference(sequence_features, conv_weight, output_grad):

    def step(weight_sum, inputs):
        xrow, grow = inputs
        length = xrow.shape[0]
        xpad = jnp.pad(xrow, ((2, 2), (0, 0)))
        pre = jnp.zeros((length, COUT), jnp.float32)
        for k in range(KW):
            pre = pre + jnp.dot(xpad[k:k + length], conv_weight[:, k * COUT:(k + 1) * COUT], preferred_element_type=jnp.float32)
        act, pull = jax.vjp(exact_gelu, pre)
        pooled = act.reshape(length // 2, 2, COUT).mean(axis=1)
        upper = jnp.repeat(grow.astype(jnp.float32), 2, axis=0) * 0.5
        pre_grad = pull(upper)[0].astype(jnp.bfloat16)
        gpad = jnp.pad(pre_grad, ((2, 2), (0, 0)))
        feature_grad = jnp.zeros((length, CIN), jnp.float32)
        blocks = []
        for k in range(KW):
            block = conv_weight[:, k * COUT:(k + 1) * COUT]
            feature_grad = feature_grad + jnp.dot(gpad[4 - k:4 - k + length], block.T, preferred_element_type=jnp.float32)
            blocks.append(jnp.dot(xpad[k:k + length].T, pre_grad, preferred_element_type=jnp.float32))
        weight_sum = weight_sum + jnp.concatenate(blocks, axis=1)
        return (weight_sum, (pooled, feature_grad))
    start = jnp.zeros((CIN, KW * COUT), jnp.float32)
    weight_grad, outs = lax.scan(step, start, (sequence_features, output_grad))
    return (outs[0], outs[1], weight_grad)
```

```python
import functools

import jax
import jax.numpy as jnp
import numpy as np
from jax import lax
from jax.experimental import pallas as pl
from jax.experimental.pallas import tpu as pltpu
from jax.sharding import Mesh
from jax.sharding import PartitionSpec as P

KW = 5
CHUNKS = ((0, 384), (384, 384), (768, 384))
F32 = jnp.float32
BF16 = jnp.bfloat16


def move(value, axes, sizes, target):
    pairs = []
    for source in np.ndindex(*sizes):
        to = target(*source)
        if to is not None:
            pairs.append(
                (
                    int(np.ravel_multi_index(source, sizes)),
                    int(np.ravel_multi_index(to, sizes)),
                )
            )
    return lax.ppermute(value, axes, pairs)


def along_y(value, step):
    return move(
        value, ("y", "c"), (4, 2), lambda y, c: ((y + (step if c else -step)) % 4, c)
    )


def other_lo(value):
    def target(lo, c, hi):
        z = (hi * 2 + lo + (-1 if c else 1)) % 4
        return (z % 2, c, z // 2)

    return move(value, ("zl", "c", "zh"), (2, 2, 2), target)


def other_core(value):
    return move(value, ("c",), (2,), lambda c: (1 - c,))


def other_hi(value):
    return move(value, ("zh",), (2,), lambda h: (1 - h,))


def along_x(value, step):
    return move(value, ("x",), (4,), lambda x: ((x + step) % 4,))


def along_seq(value, step):
    def target(h, x):
        s = h * 4 + x + step
        return (s // 4, s % 4) if 0 <= s < 8 else None

    return move(value, ("zh", "x"), (2, 4), target)


def forward_kernel(first, last, *refs):
    refs = list(refs)
    x = [refs.pop(0), refs.pop(0)]
    taps = [refs[4 * k : 4 * k + 4] for k in range(KW)]
    refs = refs[4 * KW :]
    w = jnp.concatenate([r[...] for k in range(KW) for r in taps[k]], axis=0)
    rows = 2 * x[0].shape[1]
    left = [r[k : k + 2].reshape(rows, 128) for k in range(KW) for r in x]
    left = jnp.concatenate(left, axis=1)
    total = jnp.dot(left, w, preferred_element_type=F32)
    if not first:
        total = total + refs.pop(0)[...]
    if not last:
        refs[0][...] = total
        return
    upper_ref, pooled_ref, grad_ref = refs
    half = total.shape[0] // 2
    cdf = 0.5 * (1.0 + lax.erf(total * np.float32(np.sqrt(0.5))))
    act = total * cdf
    pooled_ref[...] = (act[:half] + act[half:]) * 0.5
    pdf = jnp.exp(total * total * -0.5) * np.float32(1.0 / np.sqrt(2.0 * np.pi))
    slope = cdf + total * pdf
    upper = upper_ref[...].astype(F32) * 0.5
    grad_ref[0] = (slope[:half] * upper).astype(BF16)
    grad_ref[1] = (slope[half:] * upper).astype(BF16)


def forward_step(step, planes, pieces, acc, upper, columns, tile):
    first, last = acc is None, upper is not None
    half = planes.shape[1]
    rows, depth = 2 * half, KW * 256
    width = pieces[0].shape[1] // KW
    start, size = columns
    base, per_tap = start // tile, width // tile
    near = pl.BlockSpec((6, half, 128), lambda j: (0, 0, step))
    far = pl.BlockSpec((6, half, 128), lambda j: (0, 0, 4 + step))
    here = pl.BlockSpec((rows, tile), lambda j: (0, base + j))
    in_specs, args = [near, far], [planes, planes]
    for k in range(KW):
        for piece in pieces:
            in_specs.append(
                pl.BlockSpec((64, tile), lambda j, k=k: (0, k * per_tap + base + j))
            )
            args.append(piece)
    aliases = {}
    if not first:
        in_specs.append(here)
        args.append(acc)
        if not last:
            aliases = {len(args) - 1: 0}
    if last:
        in_specs.append(pl.BlockSpec((rows // 2, tile), lambda j: (0, base + j)))
        args.append(upper)
        out_shape = (
            jax.ShapeDtypeStruct((rows // 2, size), F32),
            jax.ShapeDtypeStruct((2, rows // 2, size), BF16),
        )
        out_specs = (
            pl.BlockSpec((rows // 2, tile), lambda j: (0, j)),
            pl.BlockSpec((2, rows // 2, tile), lambda j: (0, 0, j)),
        )
    else:
        out_shape = jax.ShapeDtypeStruct((rows, width), F32)
        out_specs = here
    return pl.pallas_call(
        functools.partial(forward_kernel, first, last),
        grid=(size // tile,),
        in_specs=in_specs,
        out_specs=out_specs,
        out_shape=out_shape,
        input_output_aliases=aliases,
        compiler_params=pltpu.CompilerParams(vmem_limit_bytes=40 << 20),
        cost_estimate=pl.CostEstimate(
            flops=2 * rows * depth * size,
            bytes_accessed=rows * depth * 2 + depth * size * 2 + rows * size * 8,
            transcendentals=2 * rows * size if last else 0,
        ),
        name="forward_last" if last else "forward_part",
    )(*args)


def back_kernel(where, grads, *refs):
    n = len(refs) - 4
    pieces, (out, whole, braid, sem) = refs[:n], refs[n:]
    copies = []
    for i in range(n):
        at = pl.ds(pl.multiple_of(where[i] * 64, 64), 64)
        copies.append(pltpu.make_async_copy(pieces[i], whole.at[at, :], sem.at[i]))
        copies[-1].start()
    for copy in copies:
        copy.wait()
    half, width = grads.shape[1:]
    tile = 256

    def body(t, carry):
        rows = pl.ds(pl.multiple_of(t * tile, tile), tile)
        total = jnp.zeros((2 * half, tile), F32)
        for k in range(KW):
            left = grads[4 - k : 6 - k].reshape(2 * half, width)
            total = total + lax.dot_general(
                left,
                whole[rows, k * width : (k + 1) * width],
                (((1,), (1,)), ((), ())),
                preferred_element_type=F32,
            )
        for u in range(tile // 128):
            lanes = slice(u * 128, (u + 1) * 128)
            braid[pl.ds(0, half, 2), :] = total[:half, lanes]
            braid[pl.ds(1, half, 2), :] = total[half:, lanes]
            at = pl.multiple_of(t * tile + u * 128, 128)
            out[:, pl.ds(at, 128)] = braid[...]
        return carry

    lax.fori_loop(0, whole.shape[0] // tile, body, 0)


def back(where, grads, pieces):
    half, width = grads.shape[1:]
    n = len(pieces)
    channels = n * 64
    return pl.pallas_call(
        back_kernel,
        in_specs=[
            pl.BlockSpec(memory_space=pltpu.SMEM),
            pl.BlockSpec(memory_space=pltpu.VMEM),
        ]
        + [pl.BlockSpec(memory_space=pl.ANY)] * n,
        out_specs=pl.BlockSpec(memory_space=pltpu.VMEM),
        out_shape=jax.ShapeDtypeStruct((2 * half, channels), F32),
        scratch_shapes=[
            pltpu.VMEM((channels, KW * width), BF16),
            pltpu.VMEM((2 * half, 128), F32),
            pltpu.SemaphoreType.DMA((n,)),
        ],
        compiler_params=pltpu.CompilerParams(vmem_limit_bytes=48 << 20),
        cost_estimate=pl.CostEstimate(
            flops=2 * 2 * half * width * KW * channels,
            bytes_accessed=channels * KW * width * 2 + 2 * half * channels * 4,
            transcendentals=0,
        ),
        name="feature_gradient",
    )(where, grads, *pieces)


def shifted(planes):
    half = planes.shape[0] - 2
    return jnp.stack([planes[m // 2 : m // 2 + half, m % 2] for m in range(6)])


def with_border(value):
    before = along_seq(value[-2:], 1)
    after = along_seq(value[:2], -1)
    return jnp.concatenate([before, value, after], axis=0)


def local(features, weights, upper):
    lo, y, c = lax.axis_index("zl"), lax.axis_index("y"), lax.axis_index("c")
    xi = lax.axis_index("x")
    features, upper = features[0], upper[0]
    positions, channels = features.shape
    half = positions // 2
    width = weights.shape[1] // KW

    near = [weights]
    for _ in range(3):
        near.append(along_y(near[-1], -1))
    far = [other_lo(p) for p in near]
    near_pair = [other_core(p) for p in near]
    far_pair = [other_core(p) for p in far]

    r = jnp.arange(channels)
    core = c ^ (r // 512)

    def channel(step, far_bit):
        row = (y + jnp.where(core == 0, -step, step)) % 4
        return (lo ^ far_bit) * 512 + row * 128 + core * 64 + r % 64

    wanted = jnp.concatenate(
        [
            channel((r // 128) % 4, (r // 64) % 2),
            channel((r // 64) % 4, (r // 256) % 2),
        ]
    )
    order = (r[:, None] == wanted[None, :]).astype(BF16)
    x = with_border(features)
    x = jnp.dot(x, order, preferred_element_type=F32).astype(BF16)
    theirs = other_core(x[:, channels + 512 :])
    spot = jnp.arange(6 * half)
    spot = 2 * (spot % half) + spot // half
    pick = (jnp.arange(positions + 4)[:, None] == spot[None, :]).astype(BF16)

    def over_positions(value, turned):
        dims = (((0,), (0,)), ((), ()))
        pair = (value, pick) if turned else (pick, value)
        return lax.dot_general(*pair, dims, preferred_element_type=F32).astype(BF16)

    planes = over_positions(x[:, :channels], False).reshape(6, half, channels)
    flat = [over_positions(v, True) for v in (x[:, channels : channels + 512], theirs)]
    tall = []
    for far_bit in (0, 1):
        rows = slice(256 * far_bit, 256 * far_bit + 256)
        taps = []
        for k in range(KW):
            lanes = slice(k * half, (k + 2) * half)
            taps.append(jnp.concatenate([v[rows, lanes] for v in flat], axis=1))
        tall.append(jnp.concatenate(taps, axis=0))

    acc = None
    for s in range(3):
        pieces = (near[s], far[s], near_pair[s], far_pair[s])
        acc = forward_step(s, planes, pieces, acc, None, (0, width), 384)
    pieces = (near[3], far[3], near_pair[3], far_pair[3])
    pooled, grads, sums = [], [], []
    for start, size in CHUNKS:
        out, grad = forward_step(3, planes, pieces, acc, upper, (start, size), 384)
        pooled.append(out)
        grads.append(grad)
        mine = grad.reshape(positions, size)
        pair = jnp.concatenate([mine, other_core(mine)], axis=0)
        given = jnp.dot(tall[1], pair, preferred_element_type=F32).astype(BF16)
        taken = other_lo(given)
        kept = jnp.dot(tall[0], pair, preferred_element_type=F32)
        kept = (kept + taken.astype(F32)).reshape(KW, 4, 64, size)
        total = kept[:, 0]
        for s in range(1, 4):
            total = total + along_y(kept[:, s].astype(BF16), s).astype(F32)
        sums.append(total)

    grad = jnp.concatenate(grads, axis=2)
    flat = grad.transpose(1, 0, 2)
    before = along_seq(flat[-1], 1)
    after = along_seq(flat[0], -1)
    flat = jnp.concatenate([before[None], flat, after[None]], axis=0)
    tops = shifted(flat)
    where = []
    for s in range(4):
        for other in (0, 1):
            cc = c ^ other
            yy = (y + jnp.where(cc == 0, -s, s)) % 4
            where += [lo * 8 + yy * 2 + cc, (1 - lo) * 8 + yy * 2 + cc]
    ordered = []
    for s in range(4):
        ordered += [near[s], far[s], near_pair[s], far_pair[s]]
    feature_grad = back(jnp.stack(where).astype(jnp.int32), tops, ordered)

    total = jnp.concatenate(sums, axis=2).reshape(KW, 4, 16, width)

    def quarter(d):
        return lax.dynamic_index_in_dim(total, (xi + d) % 4, 1, keepdims=False)

    part = quarter(0)
    for d in (1, 3, 2):
        part = part + along_x(quarter(d).astype(BF16), d).astype(F32)
    part = part + other_hi(part)
    ahead = [part] + [along_x(part, -d) for d in (1, 2, 3)]
    ring = jnp.stack(ahead + ahead)
    ring = lax.dynamic_slice_in_dim(ring, 4 - xi, 4, 0)
    weight_grad = ring.transpose(0, 2, 1, 3).reshape(64, KW * width)
    return jnp.concatenate(pooled, axis=1)[None], feature_grad[None], weight_grad


def solution(mesh):
    fine = Mesh(mesh.devices.reshape(2, 4, 2, 2, 4), ("zl", "y", "c", "zh", "x"))
    dp, seq = ("zl", "y", "c"), ("zh", "x")
    return jax.shard_map(
        local,
        mesh=fine,
        in_specs=(P(dp, seq, None), P(dp, None), P(dp, seq, None)),
        out_specs=(P(dp, seq, None), P(dp, seq, None), P(dp, None)),
        check_vma=False,
    )
```

```python
import functools

import jax
import jax.numpy as jnp
import numpy as np
from jax import lax
from jax.experimental import pallas as pl
from jax.experimental.pallas import tpu as pltpu
from jax.sharding import Mesh
from jax.sharding import PartitionSpec as P

KW = 5
SPLIT = 640
F32 = jnp.float32
BF16 = jnp.bfloat16


def move(value, axes, sizes, target):
    pairs = []
    for source in np.ndindex(*sizes):
        to = target(*source)
        if to is not None:
            pairs.append(
                (
                    int(np.ravel_multi_index(source, sizes)),
                    int(np.ravel_multi_index(to, sizes)),
                )
            )
    return lax.ppermute(value, axes, pairs)


def along_y(value, step):
    return move(
        value, ("y", "c"), (4, 2), lambda y, c: ((y + (step if c else -step)) % 4, c)
    )


def other_lo(value):
    def target(lo, c, hi):
        z = (hi * 2 + lo + (-1 if c else 1)) % 4
        return (z % 2, c, z // 2)

    return move(value, ("zl", "c", "zh"), (2, 2, 2), target)


def other_core(value):
    return move(value, ("c",), (2,), lambda c: (1 - c,))


def other_hi(value):
    return move(value, ("zh",), (2,), lambda h: (1 - h,))


def along_x(value, step):
    return move(value, ("x",), (4,), lambda x: ((x + step) % 4,))


def along_seq(value, step):
    def target(h, x):
        s = h * 4 + x + step
        return (s // 4, s % 4) if 0 <= s < 8 else None

    return move(value, ("zh", "x"), (2, 4), target)


def after(value, *others):
    return lax.optimization_barrier((value, *others))[0]


def forward_kernel(first, last, *refs):
    x, refs = refs[:4], list(refs[4:])
    taps = [refs[8 * k : 8 * k + 8] for k in range(KW)]
    refs = refs[8 * KW :]
    w = jnp.concatenate([r[...] for k in range(KW) for r in taps[k]], axis=0)
    rows = 2 * x[0].shape[1]
    left = [r[k : k + 2].reshape(rows, 128) for k in range(KW) for r in x]
    left = jnp.concatenate(left, axis=1)
    total = jnp.dot(left, w, preferred_element_type=F32)
    if not first:
        total = total + refs.pop(0)[...]
    if not last:
        refs[0][...] = total
        return
    upper_ref, pooled_ref, grad_ref = refs[0], *refs[-2:]
    half = total.shape[0] // 2
    cdf = 0.5 * (1.0 + lax.erf(total * np.float32(np.sqrt(0.5))))
    act = total * cdf
    pooled_ref[...] = (act[:half] + act[half:]) * 0.5
    pdf = jnp.exp(total * total * -0.5) * np.float32(1.0 / np.sqrt(2.0 * np.pi))
    slope = cdf + total * pdf
    upper = upper_ref[...].astype(F32) * 0.5
    grad_ref[0] = (slope[:half] * upper).astype(BF16)
    grad_ref[1] = (slope[half:] * upper).astype(BF16)


def forward_step(step, planes, pieces, acc, upper, columns, tile, pooled=None):
    first, last = acc is None, upper is not None
    half = planes.shape[1]
    rows, depth = 2 * half, KW * 512
    width = pieces[0].shape[1] // KW
    start, size = columns
    base, per_tap = start // tile, width // tile
    here = pl.BlockSpec((rows, tile), lambda j: (0, base + j))
    in_specs = [
        pl.BlockSpec((6, half, 128), lambda j, i=i: (0, 0, 2 * i + step))
        for i in range(4)
    ]
    args = [planes] * 4
    for k in range(KW):
        for piece in pieces:
            in_specs.append(
                pl.BlockSpec((64, tile), lambda j, k=k: (0, k * per_tap + base + j))
            )
            args.append(piece)
    aliases = {}
    if not first:
        in_specs.append(here)
        args.append(acc)
        if not last:
            aliases = {len(args) - 1: 0}
    if last:
        in_specs.append(pl.BlockSpec((rows // 2, tile), lambda j: (0, base + j)))
        args.append(upper)
        if pooled is not None:
            in_specs.append(pl.BlockSpec(memory_space=pl.ANY))
            args.append(pooled)
            aliases = {len(args) - 1: 0}
        out_shape = (
            jax.ShapeDtypeStruct((rows // 2, width), F32),
            jax.ShapeDtypeStruct((2, rows // 2, size), BF16),
        )
        out_specs = (
            pl.BlockSpec((rows // 2, tile), lambda j: (0, base + j)),
            pl.BlockSpec((2, rows // 2, tile), lambda j: (0, 0, j)),
        )
    else:
        out_shape = jax.ShapeDtypeStruct((rows, width), F32)
        out_specs = here
    return pl.pallas_call(
        functools.partial(forward_kernel, first, last),
        grid=(size // tile,),
        in_specs=in_specs,
        out_specs=out_specs,
        out_shape=out_shape,
        input_output_aliases=aliases,
        compiler_params=pltpu.CompilerParams(vmem_limit_bytes=24 << 20),
        cost_estimate=pl.CostEstimate(
            flops=2 * rows * depth * size,
            bytes_accessed=rows * depth * 2 + depth * size * 2 + rows * size * 8,
            transcendentals=2 * rows * size if last else 0,
        ),
        name="forward_last" if last else "forward_part",
    )(*args)


def back_kernel(first, where, grads, *refs):
    out, whole, braid, sem, out_sem = refs[-5:]
    n = whole.shape[0] // 64
    pieces = refs[:n]
    copies = []
    for i in range(n):
        at = pl.ds(pl.multiple_of(where[i] * 64, 64), 64)
        copies.append(pltpu.make_async_copy(pieces[i], whole.at[at, :], sem.at[i]))
        copies[-1].start()
    for copy in copies:
        copy.wait()
    half, width = grads.shape[1:]
    sends = []
    for t in range(n // 4):
        rows = slice(t * 256, t * 256 + 256)
        left = [grads[4 - k : 6 - k].reshape(2 * half, width) for k in range(KW)]
        total = lax.dot_general(
            jnp.concatenate(left, axis=1),
            whole[rows, :],
            (((1,), (1,)), ((), ())),
            preferred_element_type=F32,
        )
        for u in range(2):
            b = 2 * t + u
            lanes = slice(u * 128, (u + 1) * 128)
            braid[b, pl.ds(0, half, 2), :] = total[:half, lanes]
            braid[b, pl.ds(1, half, 2), :] = total[half:, lanes]
            at = pl.multiple_of(where[n + b] * 128, 128)
            to = out.at[:, pl.ds(at, 128)]
            sends.append(pltpu.make_async_copy(braid.at[b], to, out_sem.at[b]))
            sends[-1].start()
    for send in sends:
        send.wait()


def back(where, grads, pieces, earlier, channels):
    half, width = grads.shape[1:]
    n = len(pieces)
    rows = 64 * n
    args = [where, grads, *pieces]
    in_specs = [
        pl.BlockSpec(memory_space=pltpu.SMEM),
        pl.BlockSpec(memory_space=pltpu.VMEM),
    ] + [pl.BlockSpec(memory_space=pl.ANY)] * n
    aliases = {}
    if earlier is not None:
        args.append(earlier)
        in_specs.append(pl.BlockSpec(memory_space=pl.ANY))
        aliases = {n + 2: 0}
    return pl.pallas_call(
        functools.partial(back_kernel, earlier is None),
        in_specs=in_specs,
        out_specs=pl.BlockSpec(memory_space=pl.ANY),
        out_shape=jax.ShapeDtypeStruct((2 * half, channels), F32),
        input_output_aliases=aliases,
        scratch_shapes=[
            pltpu.VMEM((rows, KW * width), BF16),
            pltpu.VMEM((n // 2, 2 * half, 128), F32),
            pltpu.SemaphoreType.DMA((n,)),
            pltpu.SemaphoreType.DMA((n // 2,)),
        ],
        compiler_params=pltpu.CompilerParams(vmem_limit_bytes=16 << 20),
        cost_estimate=pl.CostEstimate(
            flops=2 * 2 * half * width * KW * rows,
            bytes_accessed=rows * KW * width * 2 + 2 * half * rows * 4,
            transcendentals=0,
        ),
        name="feature_gradient",
    )(*args)


def weight_kernel(own, theirs, mine, other, out):
    half = mine.shape[0] // 2
    taps = [slice(k * half, (k + 2) * half) for k in range(KW)]
    left = [jnp.concatenate([own[:, t], theirs[:, t]], axis=1) for t in taps]
    right = jnp.concatenate([mine[...], other[...]], axis=0)
    total = jnp.dot(jnp.concatenate(left, axis=0), right, preferred_element_type=F32)
    out[...] = total.astype(out.dtype)


def weight_part(far_bit, flat, pair, dtype):
    (positions, size), tile = pair[0].shape, 384
    rows = pl.BlockSpec((256, flat[0].shape[1]), lambda i: (far_bit, 0))
    right = pl.BlockSpec((positions, tile), lambda i: (0, i))
    return pl.pallas_call(
        weight_kernel,
        grid=(size // tile,),
        in_specs=[rows, rows, right, right],
        out_specs=pl.BlockSpec((KW * 256, tile), lambda i: (0, i)),
        out_shape=jax.ShapeDtypeStruct((KW * 256, size), dtype),
        compiler_params=pltpu.CompilerParams(vmem_limit_bytes=40 << 20),
        cost_estimate=pl.CostEstimate(
            flops=2 * KW * 256 * 2 * positions * size,
            bytes_accessed=KW * 256 * size * 4 + 4 * positions * size,
            transcendentals=0,
        ),
        name="weight_gradient",
    )(*flat, *pair)


def gathered_kernel(place, *refs):
    out = refs[-1]
    width = out.shape[1] // KW
    for d in range(4):
        rows = pl.ds(pl.multiple_of((place[0] + d) % 4 * 16, 16), 16)
        for k in range(KW):
            out[rows, k * width : (k + 1) * width] = refs[d][k]


def gathered(place, parts, width):
    vmem = pl.BlockSpec(memory_space=pltpu.VMEM)
    return pl.pallas_call(
        gathered_kernel,
        in_specs=[pl.BlockSpec(memory_space=pltpu.SMEM)] + [vmem] * 4,
        out_specs=vmem,
        out_shape=jax.ShapeDtypeStruct((64, KW * width), F32),
        name="weight_rows",
    )(place.astype(jnp.int32)[None], *parts)


def shifted(planes):
    half = planes.shape[0] - 2
    return jnp.stack([planes[m // 2 : m // 2 + half, m % 2] for m in range(6)])


def with_border(value):
    before = along_seq(value[-2:], 1)
    after = along_seq(value[:2], -1)
    return jnp.concatenate([before, value, after], axis=0)


def local(features, weights, upper):
    lo, y, c = lax.axis_index("zl"), lax.axis_index("y"), lax.axis_index("c")
    xi = lax.axis_index("x")
    features, upper = features[0], upper[0]
    positions, channels = features.shape
    half = positions // 2
    width = weights.shape[1] // KW

    r = jnp.arange(channels)
    core, far_bit = c ^ (r // 512), (r // 256) % 2
    step = (r // 64) % 4
    row = (y + jnp.where(core == 0, -step, step)) % 4
    wanted = (lo ^ far_bit) * 512 + row * 128 + core * 64 + r % 64
    order = (r[:, None] == wanted[None, :]).astype(BF16)
    features = with_border(features)
    x = jnp.dot(features, order, preferred_element_type=F32).astype(BF16)

    near = [weights, along_y(weights, -1), None, along_y(weights, -3)]
    near[1], near[3] = after((near[1], near[3]), x)
    near[2] = along_y(near[1], -1)
    far = [other_lo(near[0]), other_lo(near[1])]
    theirs = other_core(x[:, 512:])
    x = after(x, near[1], near[3])
    spot = jnp.arange(6 * half)
    spot = 2 * (spot % half) + spot // half
    pick = (jnp.arange(positions + 4)[:, None] == spot[None, :]).astype(BF16)

    def over_positions(value, turned):
        dims = (((0,), (0,)), ((), ()))
        pair = (value, pick) if turned else (pick, value)
        return lax.dot_general(*pair, dims, preferred_element_type=F32).astype(BF16)

    planes = over_positions(x, False).reshape(6, half, channels)
    far += [other_lo(p) for p in near[2:]]
    flat = [over_positions(v, True) for v in after((x[:, :512], theirs), planes)]
    planes = after(planes, far[3], *flat)
    ready = after((near[0], near[1], far[0], far[1]), far[1], planes)
    swapped = [other_core(p) for p in ready]
    near_pair, far_pair = swapped[:2], swapped[2:]

    def pieces(steps):
        return [p[s] for p in (near, far, near_pair, far_pair) for s in steps]

    acc = forward_step(0, planes, pieces((0, 1)), None, None, (0, width), 384)
    near_pair += [other_core(p) for p in near[2:]]
    far_pair += [other_core(after(far[2], acc)), other_core(far[3])]
    pooled, grad = forward_step(
        1, planes, pieces((2, 3)), acc, upper, (0, width), 384
    )
    pair = grad.reshape(positions, width)
    pair = (pair, other_core(pair))

    def quarter(value, d):
        return lax.dynamic_index_in_dim(value, (xi + d) % 4, -3, keepdims=False)

    def over_x(value, waits=()):
        got = [along_x(quarter(value, d).astype(BF16), d) for d in (1, 3, 2)]
        got = after(got, *waits)
        return sum((g.astype(F32) for g in got), quarter(value, 0).astype(F32))

    def over_y(value, waits=()):
        got = [along_y(value[..., s, :, :].astype(BF16), s) for s in (1, 3, 2)]
        got = after(got, *waits)
        return sum((g.astype(F32) for g in got), value[..., 0, :, :].astype(F32))

    def late(value):
        value = value + other_hi(value)
        got = {d: along_x(value, -d) for d in (1, 3, 2)}
        return [value, got[1], got[2], got[3]]

    def rows16(value):
        return value.reshape(KW, 4, 16, value.shape[-1])

    given = weight_part(1, flat, pair, BF16)
    taken = other_lo(given)
    kept = weight_part(0, flat, after(pair, given), F32)

    grad = after(grad, kept).transpose(1, 0, 2)
    before = along_seq(grad[-1], 1)
    behind = along_seq(grad[0], -1)
    tops = shifted(jnp.concatenate([before[None], grad, behind[None]], axis=0))

    def columns(s, earlier, waits):
        pair = (4 - s) % 4
        chip_row = (y + jnp.where(c == 0, -s, s)) % 4
        where = [c, 1 - c, 2 + c, 3 - c, lo * 4 + chip_row, (1 - lo) * 4 + chip_row]
        where = jnp.stack(where).astype(jnp.int32)
        parts = [near[s], near_pair[pair], far[s], far_pair[pair]]
        return back(where, after(tops, *waits), parts, earlier, channels)

    def rows16(value):
        return value.reshape(value.shape[0], 4, 16, value.shape[2])

    feature_grad = columns(0, None, [kept])
    for i in (1, 2):
        feature_grad = columns(i, feature_grad, [])
    kept = kept + after(taken, feature_grad).astype(F32)
    kept = kept.reshape(KW, 4, 64, width)
    first = over_y(kept[..., :SPLIT])
    second = over_x(kept[..., SPLIT:].reshape(KW, 4, 4, 16, -1))
    first, second = over_x(rows16(first)), over_y(second)
    total = jnp.concatenate([first, second], axis=2)
    feature_grad = columns(3, feature_grad, [total])
    weight_grad = gathered(xi, late(total), width)
    return pooled[None], feature_grad[None], weight_grad


def solution(mesh):
    fine = Mesh(mesh.devices.reshape(2, 4, 2, 2, 4), ("zl", "y", "c", "zh", "x"))
    dp, seq = ("zl", "y", "c"), ("zh", "x")
    return jax.shard_map(
        local,
        mesh=fine,
        in_specs=(P(dp, seq, None), P(dp, None), P(dp, seq, None)),
        out_specs=(P(dp, seq, None), P(dp, seq, None), P(dp, None)),
        check_vma=False,
    )
```

```python
import functools

import jax
import jax.numpy as jnp
import numpy as np
from jax import lax
from jax.experimental import pallas as pl
from jax.experimental.pallas import tpu as pltpu
from jax.sharding import Mesh
from jax.sharding import PartitionSpec as P

KW = 5
SPLIT = 512
F32 = jnp.float32
BF16 = jnp.bfloat16


def move(value, axes, sizes, target):
    pairs = []
    for source in np.ndindex(*sizes):
        to = target(*source)
        if to is not None:
            pairs.append(
                (
                    int(np.ravel_multi_index(source, sizes)),
                    int(np.ravel_multi_index(to, sizes)),
                )
            )
    return lax.ppermute(value, axes, pairs)


def along_y(value, step):
    return move(
        value, ("y", "c"), (4, 2), lambda y, c: ((y + (step if c else -step)) % 4, c)
    )


def other_lo(value):
    def target(lo, c, hi):
        z = (hi * 2 + lo + (-1 if c else 1)) % 4
        return (z % 2, c, z // 2)

    return move(value, ("zl", "c", "zh"), (2, 2, 2), target)


def other_core(value):
    return move(value, ("c",), (2,), lambda c: (1 - c,))


def other_hi(value):
    return move(value, ("zh",), (2,), lambda h: (1 - h,))


def along_x(value, step):
    return move(value, ("x",), (4,), lambda x: ((x + step) % 4,))


def along_seq(value, step):
    def target(h, x):
        s = h * 4 + x + step
        return (s // 4, s % 4) if 0 <= s < 8 else None

    return move(value, ("zh", "x"), (2, 4), target)


def after(value, *others):
    return lax.optimization_barrier((value, *others))[0]


def forward_kernel(first, last, *refs):
    x, refs = refs[:4], list(refs[4:])
    taps = [refs[8 * k : 8 * k + 8] for k in range(KW)]
    refs = refs[8 * KW :]
    w = jnp.concatenate([r[...] for k in range(KW) for r in taps[k]], axis=0)
    rows = 2 * x[0].shape[1]
    left = [r[k : k + 2].reshape(rows, 128) for k in range(KW) for r in x]
    left = jnp.concatenate(left, axis=1)
    total = jnp.dot(left, w, preferred_element_type=F32)
    if not first:
        total = total + refs.pop(0)[...]
    if not last:
        refs[0][...] = total
        return
    upper_ref, pooled_ref, grad_ref = refs[0], *refs[-2:]
    half = total.shape[0] // 2
    cdf = 0.5 * (1.0 + lax.erf(total * np.float32(np.sqrt(0.5))))
    act = total * cdf
    pooled_ref[...] = (act[:half] + act[half:]) * 0.5
    pdf = jnp.exp(total * total * -0.5) * np.float32(1.0 / np.sqrt(2.0 * np.pi))
    slope = cdf + total * pdf
    upper = upper_ref[...].astype(F32) * 0.5
    grad_ref[0] = (slope[:half] * upper).astype(BF16)
    grad_ref[1] = (slope[half:] * upper).astype(BF16)


def forward_step(step, planes, pieces, acc, upper, columns, tile, pooled=None):
    first, last = acc is None, upper is not None
    half = planes.shape[1]
    rows, depth = 2 * half, KW * 512
    width = pieces[0].shape[1] // KW
    start, size = columns
    base, per_tap = start // tile, width // tile
    here = pl.BlockSpec((rows, tile), lambda j: (0, base + j))
    in_specs = [
        pl.BlockSpec((6, half, 128), lambda j, i=i: (0, 0, 2 * i + step))
        for i in range(4)
    ]
    args = [planes] * 4
    for k in range(KW):
        for piece in pieces:
            in_specs.append(
                pl.BlockSpec((64, tile), lambda j, k=k: (0, k * per_tap + base + j))
            )
            args.append(piece)
    aliases = {}
    if not first:
        in_specs.append(here)
        args.append(acc)
        if not last:
            aliases = {len(args) - 1: 0}
    if last:
        in_specs.append(pl.BlockSpec((rows // 2, tile), lambda j: (0, base + j)))
        args.append(upper)
        if pooled is not None:
            in_specs.append(pl.BlockSpec(memory_space=pl.ANY))
            args.append(pooled)
            aliases = {len(args) - 1: 0}
        out_shape = (
            jax.ShapeDtypeStruct((rows // 2, width), F32),
            jax.ShapeDtypeStruct((2, rows // 2, size), BF16),
        )
        out_specs = (
            pl.BlockSpec((rows // 2, tile), lambda j: (0, base + j)),
            pl.BlockSpec((2, rows // 2, tile), lambda j: (0, 0, j)),
        )
    else:
        out_shape = jax.ShapeDtypeStruct((rows, width), F32)
        out_specs = here
    return pl.pallas_call(
        functools.partial(forward_kernel, first, last),
        grid=(size // tile,),
        in_specs=in_specs,
        out_specs=out_specs,
        out_shape=out_shape,
        input_output_aliases=aliases,
        compiler_params=pltpu.CompilerParams(vmem_limit_bytes=24 << 20),
        cost_estimate=pl.CostEstimate(
            flops=2 * rows * depth * size,
            bytes_accessed=rows * depth * 2 + depth * size * 2 + rows * size * 8,
            transcendentals=2 * rows * size if last else 0,
        ),
        name="forward_last" if last else "forward_part",
    )(*args)


def back_kernel(first, where, grads, *refs):
    out, whole, braid, sem, out_sem = refs[-5:]
    n = whole.shape[0] // 64
    pieces = refs[:n]
    copies = []
    for i in range(n):
        at = pl.ds(pl.multiple_of(where[i] * 64, 64), 64)
        copies.append(pltpu.make_async_copy(pieces[i], whole.at[at, :], sem.at[i]))
        copies[-1].start()
    for copy in copies:
        copy.wait()
    half, width = grads.shape[1:]
    sends = []
    for t in range(n // 4):
        rows = slice(t * 256, t * 256 + 256)
        left = [grads[4 - k : 6 - k].reshape(2 * half, width) for k in range(KW)]
        total = lax.dot_general(
            jnp.concatenate(left, axis=1),
            whole[rows, :],
            (((1,), (1,)), ((), ())),
            preferred_element_type=F32,
        )
        for u in range(2):
            b = 2 * t + u
            lanes = slice(u * 128, (u + 1) * 128)
            braid[b, pl.ds(0, half, 2), :] = total[:half, lanes]
            braid[b, pl.ds(1, half, 2), :] = total[half:, lanes]
            at = pl.multiple_of(where[n + b] * 128, 128)
            to = out.at[:, pl.ds(at, 128)]
            sends.append(pltpu.make_async_copy(braid.at[b], to, out_sem.at[b]))
            sends[-1].start()
    for send in sends:
        send.wait()


def back(where, grads, pieces, earlier, channels):
    half, width = grads.shape[1:]
    n = len(pieces)
    rows = 64 * n
    args = [where, grads, *pieces]
    in_specs = [
        pl.BlockSpec(memory_space=pltpu.SMEM),
        pl.BlockSpec(memory_space=pltpu.VMEM),
    ] + [pl.BlockSpec(memory_space=pl.ANY)] * n
    aliases = {}
    if earlier is not None:
        args.append(earlier)
        in_specs.append(pl.BlockSpec(memory_space=pl.ANY))
        aliases = {n + 2: 0}
    return pl.pallas_call(
        functools.partial(back_kernel, earlier is None),
        in_specs=in_specs,
        out_specs=pl.BlockSpec(memory_space=pl.ANY),
        out_shape=jax.ShapeDtypeStruct((2 * half, channels), F32),
        input_output_aliases=aliases,
        scratch_shapes=[
            pltpu.VMEM((rows, KW * width), BF16),
            pltpu.VMEM((n // 2, 2 * half, 128), F32),
            pltpu.SemaphoreType.DMA((n,)),
            pltpu.SemaphoreType.DMA((n // 2,)),
        ],
        compiler_params=pltpu.CompilerParams(vmem_limit_bytes=16 << 20),
        cost_estimate=pl.CostEstimate(
            flops=2 * 2 * half * width * KW * rows,
            bytes_accessed=rows * KW * width * 2 + 2 * half * rows * 4,
            transcendentals=0,
        ),
        name="feature_gradient",
    )(*args)


def weight_kernel(own, theirs, mine, other, out):
    half = mine.shape[0] // 2
    taps = [slice(k * half, (k + 2) * half) for k in range(KW)]
    left = [jnp.concatenate([own[:, t], theirs[:, t]], axis=1) for t in taps]
    right = jnp.concatenate([mine[...], other[...]], axis=0)
    total = jnp.dot(jnp.concatenate(left, axis=0), right, preferred_element_type=F32)
    out[...] = total.astype(out.dtype)


def weight_part(far_bit, flat, pair, dtype):
    (positions, size), tile = pair[0].shape, 384
    rows = pl.BlockSpec((256, flat[0].shape[1]), lambda i: (far_bit, 0))
    right = pl.BlockSpec((positions, tile), lambda i: (0, i))
    return pl.pallas_call(
        weight_kernel,
        grid=(size // tile,),
        in_specs=[rows, rows, right, right],
        out_specs=pl.BlockSpec((KW * 256, tile), lambda i: (0, i)),
        out_shape=jax.ShapeDtypeStruct((KW * 256, size), dtype),
        compiler_params=pltpu.CompilerParams(vmem_limit_bytes=40 << 20),
        cost_estimate=pl.CostEstimate(
            flops=2 * KW * 256 * 2 * positions * size,
            bytes_accessed=KW * 256 * size * 4 + 4 * positions * size,
            transcendentals=0,
        ),
        name="weight_gradient",
    )(*flat, *pair)


def parted_kernel(place, kept, taken, *outs):
    for k in range(KW):
        for s in range(4):
            start = (k * 4 + s) * 64
            rows = slice(start, start + 64)
            total = kept[rows, :SPLIT] + taken[rows, :SPLIT].astype(F32)
            outs[s][k] = total.astype(outs[s].dtype)
            for d in range(4):
                at = pl.multiple_of((place[0] + d) % 4 * 16 + start, 16)
                rows = pl.ds(at, 16)
                total = kept[rows, SPLIT:] + taken[rows, SPLIT:].astype(F32)
                to = slice(start // 4, start // 4 + 16)
                outs[4 + d][to, :] = total.astype(outs[4 + d].dtype)


def parted(place, kept, taken):
    vmem = pl.BlockSpec(memory_space=pltpu.VMEM)
    rest = kept.shape[1] - SPLIT
    types = (F32, BF16, BF16, BF16)
    return pl.pallas_call(
        parted_kernel,
        in_specs=[pl.BlockSpec(memory_space=pltpu.SMEM), vmem, vmem],
        out_specs=[vmem] * 8,
        out_shape=[jax.ShapeDtypeStruct((KW, 64, SPLIT), t) for t in types]
        + [jax.ShapeDtypeStruct((KW * 64, rest), t) for t in types],
        compiler_params=pltpu.CompilerParams(vmem_limit_bytes=24 << 20),
        name="partial_sums",
    )(place.astype(jnp.int32)[None], kept, taken)


def gathered_kernel(place, *refs):
    out = refs[-1]
    width = out.shape[1] // KW
    for d in range(4):
        rows = pl.ds(pl.multiple_of((place[0] + d) % 4 * 16, 16), 16)
        for k in range(KW):
            out[rows, k * width : (k + 1) * width] = refs[d][k].astype(F32)


def gathered(place, parts, width):
    vmem = pl.BlockSpec(memory_space=pltpu.VMEM)
    return pl.pallas_call(
        gathered_kernel,
        in_specs=[pl.BlockSpec(memory_space=pltpu.SMEM)] + [vmem] * 4,
        out_specs=vmem,
        out_shape=jax.ShapeDtypeStruct((64, KW * width), F32),
        name="weight_rows",
    )(place.astype(jnp.int32)[None], *parts)


def shifted(planes):
    half = planes.shape[0] - 2
    return jnp.stack([planes[m // 2 : m // 2 + half, m % 2] for m in range(6)])


def with_border(value):
    before = along_seq(value[-2:], 1)
    after = along_seq(value[:2], -1)
    return jnp.concatenate([before, value, after], axis=0)


def local(features, weights, upper):
    lo, y, c = lax.axis_index("zl"), lax.axis_index("y"), lax.axis_index("c")
    xi = lax.axis_index("x")
    features, upper = features[0], upper[0]
    positions, channels = features.shape
    half = positions // 2
    width = weights.shape[1] // KW

    r = jnp.arange(channels)
    core, far_bit = c ^ (r // 512), (r // 256) % 2
    step = (r // 64) % 4
    row = (y + jnp.where(core == 0, -step, step)) % 4
    wanted = (lo ^ far_bit) * 512 + row * 128 + core * 64 + r % 64
    order = after((r[:, None] == wanted[None, :]).astype(BF16))
    features = with_border(features)
    x = jnp.dot(features, order, preferred_element_type=F32).astype(BF16)

    near = [weights, along_y(weights, -1), None, along_y(weights, -3)]
    near[1], near[3] = after((near[1], near[3]), x)
    near[2] = along_y(near[1], -1)
    far = [other_lo(near[0]), other_lo(near[1])]
    theirs = other_core(x[:, 512:])
    x = after(x, near[1], near[3])
    spot = jnp.arange(6 * half)
    spot = 2 * (spot % half) + spot // half
    pick = after((jnp.arange(positions + 4)[:, None] == spot[None, :]).astype(BF16))

    def over_positions(value, turned):
        dims = (((0,), (0,)), ((), ()))
        pair = (value, pick) if turned else (pick, value)
        return lax.dot_general(*pair, dims, preferred_element_type=F32).astype(BF16)

    planes = over_positions(x, False).reshape(6, half, channels)
    far += [other_lo(p) for p in near[2:]]
    flat = [over_positions(v, True) for v in after((x[:, :512], theirs), planes)]
    planes = after(planes, far[3], *flat)
    ready = after((near[0], near[1], far[0], far[1]), far[1], planes)
    swapped = [other_core(p) for p in ready]
    near_pair, far_pair = swapped[:2], swapped[2:]

    def pieces(steps):
        return [p[s] for p in (near, far, near_pair, far_pair) for s in steps]

    acc = forward_step(0, planes, pieces((0, 1)), None, None, (0, width), 384)
    near_pair += [other_core(p) for p in near[2:]]
    far_pair += [other_core(after(far[2], acc)), other_core(far[3])]
    pooled, grad = forward_step(
        1, planes, pieces((2, 3)), acc, upper, (0, width), 384
    )
    pair = grad.reshape(positions, width)
    pair = (pair, other_core(pair))

    def quarter(value, d):
        return lax.dynamic_index_in_dim(value, (xi + d) % 4, -3, keepdims=False)

    def over_x(parts):
        got = [along_x(parts[d], d) for d in (1, 3, 2)]
        return got[0], sum((g.astype(F32) for g in got), parts[0])

    def over_y(parts, waits=()):
        got = [along_y(parts[s], s) for s in (1, 3, 2)]
        got = after(got, *waits) if waits else got
        return sum((g.astype(F32) for g in got), parts[0])

    def rows16(value):
        return value.reshape(KW, 4, 16, value.shape[-1])

    given = weight_part(1, flat, pair, BF16)
    taken = other_lo(given)
    kept = weight_part(0, flat, after(pair, given), F32)

    grad = after(grad, kept).transpose(1, 0, 2)
    before = along_seq(grad[-1], 1)
    behind = along_seq(grad[0], -1)
    tops = shifted(jnp.concatenate([before[None], grad, behind[None]], axis=0))

    def columns(s, earlier, waits):
        pair = (4 - s) % 4
        chip_row = (y + jnp.where(c == 0, -s, s)) % 4
        where = [c, 1 - c, 2 + c, 3 - c, lo * 4 + chip_row, (1 - lo) * 4 + chip_row]
        where = jnp.stack(where).astype(jnp.int32)
        parts = [near[s], near_pair[pair], far[s], far_pair[pair]]
        return back(where, after(tops, *waits), parts, earlier, channels)

    def rows16(value):
        return value.reshape(value.shape[0], 4, 16, value.shape[2])

    feature_grad = columns(0, None, [kept])
    feature_grad = columns(1, feature_grad, [])
    parts = parted(xi, kept, after(taken, feature_grad))
    came, second = over_x(parts[4:])
    feature_grad = columns(2, feature_grad, [came])
    first = rows16(over_y(parts[:4], [feature_grad]))
    _, first = over_x([quarter(first, d) for d in range(4)])
    second = second.reshape(KW, 4, 16, -1)
    second = over_y([second[:, s] for s in range(4)])
    total = jnp.concatenate([first, second], axis=2)

    total = total + other_hi(total)
    total = total.astype(BF16)
    feature_grad = columns(3, feature_grad, [total])
    got = {d: along_x(total, -d) for d in (1, 3, 2)}
    weight_grad = gathered(xi, [total, got[1], got[2], got[3]], width)
    return pooled[None], feature_grad[None], weight_grad


def solution(mesh):
    fine = Mesh(mesh.devices.reshape(2, 4, 2, 2, 4), ("zl", "y", "c", "zh", "x"))
    dp, seq = ("zl", "y", "c"), ("zh", "x")
    return jax.shard_map(
        local,
        mesh=fine,
        in_specs=(P(dp, seq, None), P(dp, None), P(dp, seq, None)),
        out_specs=(P(dp, seq, None), P(dp, seq, None), P(dp, None)),
        check_vma=False,
    )
```

```python
import functools

import jax
import jax.numpy as jnp
import numpy as np
from jax import lax
from jax.experimental import pallas as pl
from jax.experimental.pallas import tpu as pltpu
from jax.sharding import Mesh
from jax.sharding import PartitionSpec as P

KW = 5
SPLIT = 512
F32 = jnp.float32
BF16 = jnp.bfloat16


def move(value, axes, sizes, target):
    pairs = []
    for source in np.ndindex(*sizes):
        to = target(*source)
        if to is not None:
            pairs.append(
                (
                    int(np.ravel_multi_index(source, sizes)),
                    int(np.ravel_multi_index(to, sizes)),
                )
            )
    return lax.ppermute(value, axes, pairs)


def along_y(value, step):
    return move(
        value, ("y", "c"), (4, 2), lambda y, c: ((y + (step if c else -step)) % 4, c)
    )


def other_lo(value):
    def target(lo, c, hi):
        z = (hi * 2 + lo + (-1 if c else 1)) % 4
        return (z % 2, c, z // 2)

    return move(value, ("zl", "c", "zh"), (2, 2, 2), target)


def other_core(value):
    return move(value, ("c",), (2,), lambda c: (1 - c,))


def other_hi(value):
    return move(value, ("zh",), (2,), lambda h: (1 - h,))


def along_x(value, step):
    return move(value, ("x",), (4,), lambda x: ((x + step) % 4,))


def along_seq(value, step):
    def target(h, x):
        s = h * 4 + x + step
        return (s // 4, s % 4) if 0 <= s < 8 else None

    return move(value, ("zh", "x"), (2, 4), target)


def after(value, *others):
    return lax.optimization_barrier((value, *others))[0]


def forward_kernel(first, last, *refs):
    x, refs = refs[:4], list(refs[4:])
    taps = [refs[8 * k : 8 * k + 8] for k in range(KW)]
    refs = refs[8 * KW :]
    w = jnp.concatenate([r[...] for k in range(KW) for r in taps[k]], axis=0)
    rows = 2 * x[0].shape[1]
    left = [r[k : k + 2].reshape(rows, 128) for k in range(KW) for r in x]
    left = jnp.concatenate(left, axis=1)
    total = jnp.dot(left, w, preferred_element_type=F32)
    if not first:
        total = total + refs.pop(0)[...]
    if not last:
        refs[0][...] = total
        return
    upper_ref, pooled_ref, grad_ref = refs[0], *refs[-2:]
    half = total.shape[0] // 2
    cdf = 0.5 * (1.0 + lax.erf(total * np.float32(np.sqrt(0.5))))
    act = total * cdf
    pooled_ref[...] = (act[:half] + act[half:]) * 0.5
    pdf = jnp.exp(total * total * -0.5) * np.float32(1.0 / np.sqrt(2.0 * np.pi))
    slope = cdf + total * pdf
    upper = upper_ref[...].astype(F32) * 0.5
    grad_ref[0] = (slope[:half] * upper).astype(BF16)
    grad_ref[1] = (slope[half:] * upper).astype(BF16)


def forward_step(step, planes, pieces, acc, upper, columns, tile, pooled=None):
    first, last = acc is None, upper is not None
    half = planes.shape[1]
    rows, depth = 2 * half, KW * 512
    width = pieces[0].shape[1] // KW
    start, size = columns
    base, per_tap = start // tile, width // tile
    here = pl.BlockSpec((rows, tile), lambda j: (0, base + j))
    in_specs = [
        pl.BlockSpec((6, half, 128), lambda j, i=i: (0, 0, 2 * i + step))
        for i in range(4)
    ]
    args = [planes] * 4
    for k in range(KW):
        for piece in pieces:
            in_specs.append(
                pl.BlockSpec((64, tile), lambda j, k=k: (0, k * per_tap + base + j))
            )
            args.append(piece)
    aliases = {}
    if not first:
        in_specs.append(here)
        args.append(acc)
        if not last:
            aliases = {len(args) - 1: 0}
    if last:
        in_specs.append(pl.BlockSpec((rows // 2, tile), lambda j: (0, base + j)))
        args.append(upper)
        if pooled is not None:
            in_specs.append(pl.BlockSpec(memory_space=pl.ANY))
            args.append(pooled)
            aliases = {len(args) - 1: 0}
        out_shape = (
            jax.ShapeDtypeStruct((rows // 2, width), F32),
            jax.ShapeDtypeStruct((2, rows // 2, size), BF16),
        )
        out_specs = (
            pl.BlockSpec((rows // 2, tile), lambda j: (0, base + j)),
            pl.BlockSpec((2, rows // 2, tile), lambda j: (0, 0, j)),
        )
    else:
        out_shape = jax.ShapeDtypeStruct((rows, width), F32)
        out_specs = here
    return pl.pallas_call(
        functools.partial(forward_kernel, first, last),
        grid=(size // tile,),
        in_specs=in_specs,
        out_specs=out_specs,
        out_shape=out_shape,
        input_output_aliases=aliases,
        compiler_params=pltpu.CompilerParams(vmem_limit_bytes=24 << 20),
        cost_estimate=pl.CostEstimate(
            flops=2 * rows * depth * size,
            bytes_accessed=rows * depth * 2 + depth * size * 2 + rows * size * 8,
            transcendentals=2 * rows * size if last else 0,
        ),
        name="forward_last" if last else "forward_part",
    )(*args)


def back_kernel(first, where, grads, *refs):
    out, whole, braid, sem, out_sem = refs[-5:]
    n = whole.shape[0] // 64
    pieces = refs[:n]
    copies = []
    for i in range(n):
        at = pl.ds(pl.multiple_of(where[i] * 64, 64), 64)
        copies.append(pltpu.make_async_copy(pieces[i], whole.at[at, :], sem.at[i]))
        copies[-1].start()
    for copy in copies:
        copy.wait()
    half, width = grads.shape[1:]
    sends = []
    for t in range(n // 4):
        rows = slice(t * 256, t * 256 + 256)
        left = [grads[4 - k : 6 - k].reshape(2 * half, width) for k in range(KW)]
        total = lax.dot_general(
            jnp.concatenate(left, axis=1),
            whole[rows, :],
            (((1,), (1,)), ((), ())),
            preferred_element_type=F32,
        )
        for u in range(2):
            b = 2 * t + u
            lanes = slice(u * 128, (u + 1) * 128)
            braid[b, pl.ds(0, half, 2), :] = total[:half, lanes]
            braid[b, pl.ds(1, half, 2), :] = total[half:, lanes]
            at = pl.multiple_of(where[n + b] * 128, 128)
            to = out.at[:, pl.ds(at, 128)]
            sends.append(pltpu.make_async_copy(braid.at[b], to, out_sem.at[b]))
            sends[-1].start()
    for send in sends:
        send.wait()


def back(where, grads, pieces, earlier, channels):
    half, width = grads.shape[1:]
    n = len(pieces)
    rows = 64 * n
    args = [where, grads, *pieces]
    in_specs = [
        pl.BlockSpec(memory_space=pltpu.SMEM),
        pl.BlockSpec(memory_space=pltpu.VMEM),
    ] + [pl.BlockSpec(memory_space=pl.ANY)] * n
    aliases = {}
    if earlier is not None:
        args.append(earlier)
        in_specs.append(pl.BlockSpec(memory_space=pl.ANY))
        aliases = {n + 2: 0}
    return pl.pallas_call(
        functools.partial(back_kernel, earlier is None),
        in_specs=in_specs,
        out_specs=pl.BlockSpec(memory_space=pl.ANY),
        out_shape=jax.ShapeDtypeStruct((2 * half, channels), F32),
        input_output_aliases=aliases,
        scratch_shapes=[
            pltpu.VMEM((rows, KW * width), BF16),
            pltpu.VMEM((n // 2, 2 * half, 128), F32),
            pltpu.SemaphoreType.DMA((n,)),
            pltpu.SemaphoreType.DMA((n // 2,)),
        ],
        compiler_params=pltpu.CompilerParams(vmem_limit_bytes=16 << 20),
        cost_estimate=pl.CostEstimate(
            flops=2 * 2 * half * width * KW * rows,
            bytes_accessed=rows * KW * width * 2 + 2 * half * rows * 4,
            transcendentals=0,
        ),
        name="feature_gradient",
    )(*args)


def weight_kernel(own, theirs, mine, other, out):
    half = mine.shape[0] // 2
    taps = [slice(k * half, (k + 2) * half) for k in range(KW)]
    left = [jnp.concatenate([own[:, t], theirs[:, t]], axis=1) for t in taps]
    right = jnp.concatenate([mine[...], other[...]], axis=0)
    total = jnp.dot(jnp.concatenate(left, axis=0), right, preferred_element_type=F32)
    out[...] = total.astype(out.dtype)


def weight_part(far_bit, flat, pair, dtype):
    (positions, size), tile = pair[0].shape, 384
    rows = pl.BlockSpec((256, flat[0].shape[1]), lambda i: (far_bit, 0))
    right = pl.BlockSpec((positions, tile), lambda i: (0, i))
    return pl.pallas_call(
        weight_kernel,
        grid=(size // tile,),
        in_specs=[rows, rows, right, right],
        out_specs=pl.BlockSpec((KW * 256, tile), lambda i: (0, i)),
        out_shape=jax.ShapeDtypeStruct((KW * 256, size), dtype),
        compiler_params=pltpu.CompilerParams(vmem_limit_bytes=40 << 20),
        cost_estimate=pl.CostEstimate(
            flops=2 * KW * 256 * 2 * positions * size,
            bytes_accessed=KW * 256 * size * 4 + 4 * positions * size,
            transcendentals=0,
        ),
        name="weight_gradient",
    )(*flat, *pair)


def parted_kernel(place, kept, taken, *outs):
    for k in range(KW):
        for s in range(4):
            start = (k * 4 + s) * 64
            rows = slice(start, start + 64)
            total = kept[rows, :SPLIT] + taken[rows, :SPLIT].astype(F32)
            outs[s][k] = total.astype(outs[s].dtype)
            for d in range(4):
                at = pl.multiple_of((place[0] + d) % 4 * 16 + start, 16)
                rows = pl.ds(at, 16)
                total = kept[rows, SPLIT:] + taken[rows, SPLIT:].astype(F32)
                to = slice(start // 4, start // 4 + 16)
                outs[4 + d][to, :] = total.astype(outs[4 + d].dtype)


def parted(place, kept, taken):
    vmem = pl.BlockSpec(memory_space=pltpu.VMEM)
    rest = kept.shape[1] - SPLIT
    types = (F32, BF16, BF16, BF16)
    return pl.pallas_call(
        parted_kernel,
        in_specs=[pl.BlockSpec(memory_space=pltpu.SMEM), vmem, vmem],
        out_specs=[vmem] * 8,
        out_shape=[jax.ShapeDtypeStruct((KW, 64, SPLIT), t) for t in types]
        + [jax.ShapeDtypeStruct((KW * 64, rest), t) for t in types],
        compiler_params=pltpu.CompilerParams(vmem_limit_bytes=24 << 20),
        name="partial_sums",
    )(place.astype(jnp.int32)[None], kept, taken)


def gathered_kernel(place, *refs):
    out = refs[-1]
    width = out.shape[1] // KW
    for d in range(4):
        rows = pl.ds(pl.multiple_of((place[0] + d) % 4 * 16, 16), 16)
        for k in range(KW):
            start = k * width
            out[rows, start : start + SPLIT] = refs[d][k].astype(F32)
            out[rows, start + SPLIT : start + width] = refs[4 + d][k].astype(F32)


def gathered(place, parts, width):
    vmem = pl.BlockSpec(memory_space=pltpu.VMEM)
    return pl.pallas_call(
        gathered_kernel,
        in_specs=[pl.BlockSpec(memory_space=pltpu.SMEM)] + [vmem] * 8,
        out_specs=vmem,
        out_shape=jax.ShapeDtypeStruct((64, KW * width), F32),
        name="weight_rows",
    )(place.astype(jnp.int32)[None], *parts)


def shifted(planes):
    half = planes.shape[0] - 2
    return jnp.stack([planes[m // 2 : m // 2 + half, m % 2] for m in range(6)])


def with_border(value):
    before = along_seq(value[-2:], 1)
    after = along_seq(value[:2], -1)
    return jnp.concatenate([before, value, after], axis=0)


def local(features, weights, upper):
    lo, y, c = lax.axis_index("zl"), lax.axis_index("y"), lax.axis_index("c")
    xi = lax.axis_index("x")
    features, upper = features[0], upper[0]
    positions, channels = features.shape
    half = positions // 2
    width = weights.shape[1] // KW

    r = jnp.arange(channels)
    core, far_bit = c ^ (r // 512), (r // 256) % 2
    step = (r // 64) % 4
    row = (y + jnp.where(core == 0, -step, step)) % 4
    wanted = (lo ^ far_bit) * 512 + row * 128 + core * 64 + r % 64
    order = after((r[:, None] == wanted[None, :]).astype(BF16))
    features = with_border(features)
    x = jnp.dot(features, order, preferred_element_type=F32).astype(BF16)

    near = [weights, along_y(weights, -1), None, along_y(weights, -3)]
    near[1], near[3] = after((near[1], near[3]), x)
    near[2] = along_y(near[1], -1)
    far = [other_lo(near[0]), other_lo(near[1])]
    theirs = other_core(x[:, 512:])
    x = after(x, near[1], near[3])
    spot = jnp.arange(6 * half)
    spot = 2 * (spot % half) + spot // half
    pick = after((jnp.arange(positions + 4)[:, None] == spot[None, :]).astype(BF16))

    def over_positions(value, turned):
        dims = (((0,), (0,)), ((), ()))
        pair = (value, pick) if turned else (pick, value)
        return lax.dot_general(*pair, dims, preferred_element_type=F32).astype(BF16)

    planes = over_positions(x, False).reshape(6, half, channels)
    far += [other_lo(p) for p in near[2:]]
    flat = [over_positions(v, True) for v in after((x[:, :512], theirs), planes)]
    planes = after(planes, far[3], *flat)
    ready = after((near[0], near[1], far[0], far[1]), far[1], planes)
    swapped = [other_core(p) for p in ready]
    near_pair, far_pair = swapped[:2], swapped[2:]

    def pieces(steps):
        return [p[s] for p in (near, far, near_pair, far_pair) for s in steps]

    acc = forward_step(0, planes, pieces((0, 1)), None, None, (0, width), 384)
    near_pair += [other_core(p) for p in near[2:]]
    far_pair += [other_core(after(far[2], acc)), other_core(far[3])]
    pooled, grad = forward_step(
        1, planes, pieces((2, 3)), acc, upper, (0, width), 384
    )
    pair = grad.reshape(positions, width)
    pair = (pair, other_core(pair))

    def quarter(value, d):
        return lax.dynamic_index_in_dim(value, (xi + d) % 4, -3, keepdims=False)

    def over_x(parts):
        got = [along_x(parts[d], d) for d in (1, 3, 2)]
        return got[0], sum((g.astype(F32) for g in got), parts[0])

    def over_y(parts, waits=()):
        got = [along_y(parts[s], s) for s in (1, 3, 2)]
        got = after(got, *waits) if waits else got
        return sum((g.astype(F32) for g in got), parts[0])

    def rows16(value):
        return value.reshape(KW, 4, 16, value.shape[-1])

    given = weight_part(1, flat, pair, BF16)
    taken = other_lo(given)
    kept = weight_part(0, flat, after(pair, given), F32)

    grad = after(grad, kept).transpose(1, 0, 2)
    before = along_seq(grad[-1], 1)
    behind = along_seq(grad[0], -1)
    tops = shifted(jnp.concatenate([before[None], grad, behind[None]], axis=0))

    def columns(s, earlier, waits):
        pair = (4 - s) % 4
        chip_row = (y + jnp.where(c == 0, -s, s)) % 4
        where = [c, 1 - c, 2 + c, 3 - c, lo * 4 + chip_row, (1 - lo) * 4 + chip_row]
        where = jnp.stack(where).astype(jnp.int32)
        parts = [near[s], near_pair[pair], far[s], far_pair[pair]]
        return back(where, after(tops, *waits), parts, earlier, channels)

    def rows16(value):
        return value.reshape(value.shape[0], 4, 16, value.shape[2])

    feature_grad = columns(0, None, [kept])
    feature_grad = columns(1, feature_grad, [])
    parts = parted(xi, kept, after(taken, feature_grad))
    came, second = over_x(parts[4:])
    feature_grad = columns(2, feature_grad, [came])
    first = rows16(over_y(parts[:4], [feature_grad]))
    _, first = over_x([quarter(first, d) for d in range(4)])
    second = second.reshape(KW, 4, 16, -1)
    second = over_y([second[:, s] for s in range(4)])

    first = (first + other_hi(first)).astype(BF16)
    second = (second + other_hi(second)).astype(BF16)
    feature_grad = columns(3, feature_grad, [second])
    rows = []
    for value in (first, second):
        got = {d: along_x(value, -d) for d in (1, 3, 2)}
        rows += [value, got[1], got[2], got[3]]
    weight_grad = gathered(xi, rows, width)
    return pooled[None], feature_grad[None], weight_grad


def solution(mesh):
    fine = Mesh(mesh.devices.reshape(2, 4, 2, 2, 4), ("zl", "y", "c", "zh", "x"))
    dp, seq = ("zl", "y", "c"), ("zh", "x")
    return jax.shard_map(
        local,
        mesh=fine,
        in_specs=(P(dp, seq, None), P(dp, None), P(dp, seq, None)),
        out_specs=(P(dp, seq, None), P(dp, seq, None), P(dp, None)),
        check_vma=False,
    )
```

```python
import functools

import jax
import jax.numpy as jnp
import numpy as np
from jax import lax
from jax.experimental import pallas as pl
from jax.experimental.pallas import tpu as pltpu
from jax.sharding import Mesh
from jax.sharding import PartitionSpec as P

KW = 5
SPLIT = 640
F32 = jnp.float32
BF16 = jnp.bfloat16


def move(value, axes, sizes, target):
    pairs = []
    for source in np.ndindex(*sizes):
        to = target(*source)
        if to is not None:
            pairs.append(
                (
                    int(np.ravel_multi_index(source, sizes)),
                    int(np.ravel_multi_index(to, sizes)),
                )
            )
    return lax.ppermute(value, axes, pairs)


def along_y(value, step):
    return move(
        value, ("y", "c"), (4, 2), lambda y, c: ((y + (step if c else -step)) % 4, c)
    )


def other_lo(value):
    def target(lo, c, hi):
        z = (hi * 2 + lo + (-1 if c else 1)) % 4
        return (z % 2, c, z // 2)

    return move(value, ("zl", "c", "zh"), (2, 2, 2), target)


def other_core(value):
    return move(value, ("c",), (2,), lambda c: (1 - c,))


def other_hi(value):
    return move(value, ("zh",), (2,), lambda h: (1 - h,))


def along_x(value, step):
    return move(value, ("x",), (4,), lambda x: ((x + step) % 4,))


def along_seq(value, step):
    def target(h, x):
        s = h * 4 + x + step
        return (s // 4, s % 4) if 0 <= s < 8 else None

    return move(value, ("zh", "x"), (2, 4), target)


def after(value, *others):
    return lax.optimization_barrier((value, *others))[0]


def forward_kernel(first, last, *refs):
    x, refs = refs[:4], list(refs[4:])
    taps = [refs[8 * k : 8 * k + 8] for k in range(KW)]
    refs = refs[8 * KW :]
    w = jnp.concatenate([r[...] for k in range(KW) for r in taps[k]], axis=0)
    rows = 2 * x[0].shape[1]
    left = [r[k : k + 2].reshape(rows, 128) for k in range(KW) for r in x]
    left = jnp.concatenate(left, axis=1)
    total = jnp.dot(left, w, preferred_element_type=F32)
    if not first:
        total = total + refs.pop(0)[...]
    if not last:
        refs[0][...] = total
        return
    upper_ref, pooled_ref, grad_ref = refs[0], *refs[-2:]
    half = total.shape[0] // 2
    cdf = 0.5 * (1.0 + lax.erf(total * np.float32(np.sqrt(0.5))))
    act = total * cdf
    pooled_ref[...] = (act[:half] + act[half:]) * 0.5
    pdf = jnp.exp(total * total * -0.5) * np.float32(1.0 / np.sqrt(2.0 * np.pi))
    slope = cdf + total * pdf
    upper = upper_ref[...].astype(F32) * 0.5
    grad_ref[0] = (slope[:half] * upper).astype(BF16)
    grad_ref[1] = (slope[half:] * upper).astype(BF16)


def forward_step(step, planes, pieces, acc, upper, columns, tile, pooled=None):
    first, last = acc is None, upper is not None
    half = planes.shape[1]
    rows, depth = 2 * half, KW * 512
    width = pieces[0].shape[1] // KW
    start, size = columns
    base, per_tap = start // tile, width // tile
    here = pl.BlockSpec((rows, tile), lambda j: (0, base + j))
    in_specs = [
        pl.BlockSpec((6, half, 128), lambda j, i=i: (0, 0, 2 * i + step))
        for i in range(4)
    ]
    args = [planes] * 4
    for k in range(KW):
        for piece in pieces:
            in_specs.append(
                pl.BlockSpec((64, tile), lambda j, k=k: (0, k * per_tap + base + j))
            )
            args.append(piece)
    aliases = {}
    if not first:
        in_specs.append(here)
        args.append(acc)
        if not last:
            aliases = {len(args) - 1: 0}
    if last:
        in_specs.append(pl.BlockSpec((rows // 2, tile), lambda j: (0, base + j)))
        args.append(upper)
        if pooled is not None:
            in_specs.append(pl.BlockSpec(memory_space=pl.ANY))
            args.append(pooled)
            aliases = {len(args) - 1: 0}
        out_shape = (
            jax.ShapeDtypeStruct((rows // 2, width), F32),
            jax.ShapeDtypeStruct((2, rows // 2, size), BF16),
        )
        out_specs = (
            pl.BlockSpec((rows // 2, tile), lambda j: (0, base + j)),
            pl.BlockSpec((2, rows // 2, tile), lambda j: (0, 0, j)),
        )
    else:
        out_shape = jax.ShapeDtypeStruct((rows, width), F32)
        out_specs = here
    return pl.pallas_call(
        functools.partial(forward_kernel, first, last),
        grid=(size // tile,),
        in_specs=in_specs,
        out_specs=out_specs,
        out_shape=out_shape,
        input_output_aliases=aliases,
        compiler_params=pltpu.CompilerParams(vmem_limit_bytes=24 << 20),
        cost_estimate=pl.CostEstimate(
            flops=2 * rows * depth * size,
            bytes_accessed=rows * depth * 2 + depth * size * 2 + rows * size * 8,
            transcendentals=2 * rows * size if last else 0,
        ),
        name="forward_last" if last else "forward_part",
    )(*args)


def back_kernel(first, where, grads, *refs):
    out, whole, braid, sem, out_sem = refs[-5:]
    n = whole.shape[0] // 64
    pieces = refs[:n]
    copies = []
    for i in range(n):
        at = pl.ds(pl.multiple_of(where[i] * 64, 64), 64)
        copies.append(pltpu.make_async_copy(pieces[i], whole.at[at, :], sem.at[i]))
        copies[-1].start()
    for copy in copies:
        copy.wait()
    half, width = grads.shape[1:]
    sends = []
    for t in range(n // 4):
        rows = slice(t * 256, t * 256 + 256)
        left = [grads[4 - k : 6 - k].reshape(2 * half, width) for k in range(KW)]
        total = lax.dot_general(
            jnp.concatenate(left, axis=1),
            whole[rows, :],
            (((1,), (1,)), ((), ())),
            preferred_element_type=F32,
        )
        for u in range(2):
            b = 2 * t + u
            lanes = slice(u * 128, (u + 1) * 128)
            braid[b, pl.ds(0, half, 2), :] = total[:half, lanes]
            braid[b, pl.ds(1, half, 2), :] = total[half:, lanes]
            at = pl.multiple_of(where[n + b] * 128, 128)
            to = out.at[:, pl.ds(at, 128)]
            sends.append(pltpu.make_async_copy(braid.at[b], to, out_sem.at[b]))
            sends[-1].start()
    for send in sends:
        send.wait()


def back(where, grads, pieces, earlier, channels):
    half, width = grads.shape[1:]
    n = len(pieces)
    rows = 64 * n
    args = [where, grads, *pieces]
    in_specs = [
        pl.BlockSpec(memory_space=pltpu.SMEM),
        pl.BlockSpec(memory_space=pltpu.VMEM),
    ] + [pl.BlockSpec(memory_space=pl.ANY)] * n
    aliases = {}
    if earlier is not None:
        args.append(earlier)
        in_specs.append(pl.BlockSpec(memory_space=pl.ANY))
        aliases = {n + 2: 0}
    return pl.pallas_call(
        functools.partial(back_kernel, earlier is None),
        in_specs=in_specs,
        out_specs=pl.BlockSpec(memory_space=pl.ANY),
        out_shape=jax.ShapeDtypeStruct((2 * half, channels), F32),
        input_output_aliases=aliases,
        scratch_shapes=[
            pltpu.VMEM((rows, KW * width), BF16),
            pltpu.VMEM((n // 2, 2 * half, 128), F32),
            pltpu.SemaphoreType.DMA((n,)),
            pltpu.SemaphoreType.DMA((n // 2,)),
        ],
        compiler_params=pltpu.CompilerParams(vmem_limit_bytes=16 << 20),
        cost_estimate=pl.CostEstimate(
            flops=2 * 2 * half * width * KW * rows,
            bytes_accessed=rows * KW * width * 2 + 2 * half * rows * 4,
            transcendentals=0,
        ),
        name="feature_gradient",
    )(*args)


def weight_kernel(own, theirs, mine, other, out):
    half = mine.shape[0] // 2
    taps = [slice(k * half, (k + 2) * half) for k in range(KW)]
    left = [jnp.concatenate([own[:, t], theirs[:, t]], axis=1) for t in taps]
    right = jnp.concatenate([mine[...], other[...]], axis=0)
    total = jnp.dot(jnp.concatenate(left, axis=0), right, preferred_element_type=F32)
    out[...] = total.astype(out.dtype)


def weight_part(far_bit, flat, pair, dtype):
    (positions, size), tile = pair[0].shape, 384
    rows = pl.BlockSpec((256, flat[0].shape[1]), lambda i: (far_bit, 0))
    right = pl.BlockSpec((positions, tile), lambda i: (0, i))
    return pl.pallas_call(
        weight_kernel,
        grid=(size // tile,),
        in_specs=[rows, rows, right, right],
        out_specs=pl.BlockSpec((KW * 256, tile), lambda i: (0, i)),
        out_shape=jax.ShapeDtypeStruct((KW * 256, size), dtype),
        compiler_params=pltpu.CompilerParams(vmem_limit_bytes=40 << 20),
        cost_estimate=pl.CostEstimate(
            flops=2 * KW * 256 * 2 * positions * size,
            bytes_accessed=KW * 256 * size * 4 + 4 * positions * size,
            transcendentals=0,
        ),
        name="weight_gradient",
    )(*flat, *pair)


def parted_kernel(place, kept, taken, *outs):
    for k in range(KW):
        for s in range(4):
            start = (k * 4 + s) * 64
            rows = slice(start, start + 64)
            total = kept[rows, :SPLIT] + taken[rows, :SPLIT].astype(F32)
            outs[s][k] = total.astype(outs[s].dtype)
            for d in range(4):
                at = pl.multiple_of((place[0] + d) % 4 * 16 + start, 16)
                rows = pl.ds(at, 16)
                total = kept[rows, SPLIT:] + taken[rows, SPLIT:].astype(F32)
                to = slice(start // 4, start // 4 + 16)
                outs[4 + d][to, :] = total.astype(outs[4 + d].dtype)


def parted(place, kept, taken):
    vmem = pl.BlockSpec(memory_space=pltpu.VMEM)
    rest = kept.shape[1] - SPLIT
    types = (F32, BF16, BF16, BF16)
    return pl.pallas_call(
        parted_kernel,
        in_specs=[pl.BlockSpec(memory_space=pltpu.SMEM), vmem, vmem],
        out_specs=[vmem] * 8,
        out_shape=[jax.ShapeDtypeStruct((KW, 64, SPLIT), t) for t in types]
        + [jax.ShapeDtypeStruct((KW * 64, rest), t) for t in types],
        compiler_params=pltpu.CompilerParams(vmem_limit_bytes=24 << 20),
        name="partial_sums",
    )(place.astype(jnp.int32)[None], kept, taken)


def gathered_kernel(place, *refs):
    out = refs[-1]
    width = out.shape[1] // KW
    for d in range(4):
        rows = pl.ds(pl.multiple_of((place[0] + d) % 4 * 16, 16), 16)
        for k in range(KW):
            start = k * width
            out[rows, start : start + SPLIT] = refs[d][k].astype(F32)
            out[rows, start + SPLIT : start + width] = refs[4 + d][k].astype(F32)


def gathered(place, parts, width):
    vmem = pl.BlockSpec(memory_space=pltpu.VMEM)
    return pl.pallas_call(
        gathered_kernel,
        in_specs=[pl.BlockSpec(memory_space=pltpu.SMEM)] + [vmem] * 8,
        out_specs=vmem,
        out_shape=jax.ShapeDtypeStruct((64, KW * width), F32),
        name="weight_rows",
    )(place.astype(jnp.int32)[None], *parts)


def shifted(planes):
    half = planes.shape[0] - 2
    return jnp.stack([planes[m // 2 : m // 2 + half, m % 2] for m in range(6)])


def with_border(value):
    before = along_seq(value[-2:], 1)
    after = along_seq(value[:2], -1)
    return jnp.concatenate([before, value, after], axis=0)


def local(features, weights, upper):
    lo, y, c = lax.axis_index("zl"), lax.axis_index("y"), lax.axis_index("c")
    xi = lax.axis_index("x")
    features, upper = features[0], upper[0]
    positions, channels = features.shape
    half = positions // 2
    width = weights.shape[1] // KW

    r = jnp.arange(channels)
    core, far_bit = c ^ (r // 512), (r // 256) % 2
    step = (r // 64) % 4
    row = (y + jnp.where(core == 0, -step, step)) % 4
    wanted = (lo ^ far_bit) * 512 + row * 128 + core * 64 + r % 64
    order = after((r[:, None] == wanted[None, :]).astype(BF16))
    features = with_border(features)
    x = jnp.dot(features, order, preferred_element_type=F32).astype(BF16)

    near = [weights, along_y(weights, -1), None, along_y(weights, -3)]
    near[1], near[3] = after((near[1], near[3]), x)
    near[2] = along_y(near[1], -1)
    far = [other_lo(near[0]), other_lo(near[1])]
    theirs = other_core(x[:, 512:])
    x = after(x, near[1], near[3])
    spot = jnp.arange(6 * half)
    spot = 2 * (spot % half) + spot // half
    pick = after((jnp.arange(positions + 4)[:, None] == spot[None, :]).astype(BF16))

    def over_positions(value, turned):
        dims = (((0,), (0,)), ((), ()))
        pair = (value, pick) if turned else (pick, value)
        return lax.dot_general(*pair, dims, preferred_element_type=F32).astype(BF16)

    planes = over_positions(x, False).reshape(6, half, channels)
    far += [other_lo(p) for p in near[2:]]
    flat = [over_positions(v, True) for v in after((x[:, :512], theirs), planes)]
    planes = after(planes, far[3], *flat)
    ready = after((near[0], near[1], far[0], far[1]), far[1], planes)
    swapped = [other_core(p) for p in ready]
    near_pair, far_pair = swapped[:2], swapped[2:]

    def pieces(steps):
        return [p[s] for p in (near, far, near_pair, far_pair) for s in steps]

    acc = forward_step(0, planes, pieces((0, 1)), None, None, (0, width), 384)
    near_pair += [other_core(p) for p in near[2:]]
    far_pair += [other_core(after(far[2], acc)), other_core(far[3])]
    pooled, grad = forward_step(
        1, planes, pieces((2, 3)), acc, upper, (0, width), 384
    )
    pair = grad.reshape(positions, width)
    pair = (pair, other_core(pair))

    def quarter(value, d):
        return lax.dynamic_index_in_dim(value, (xi + d) % 4, -3, keepdims=False)

    def over_x(parts):
        got = [along_x(parts[d], d) for d in (1, 3, 2)]
        return got[0], sum((g.astype(F32) for g in got), parts[0])

    def over_y(parts, waits=()):
        got = [along_y(parts[s], s) for s in (1, 3, 2)]
        got = after(got, *waits) if waits else got
        return sum((g.astype(F32) for g in got), parts[0])

    def rows16(value):
        return value.reshape(KW, 4, 16, value.shape[-1])

    given = weight_part(1, flat, pair, BF16)
    taken = other_lo(given)
    kept = weight_part(0, flat, after(pair, given), F32)

    grad = after(grad, kept).transpose(1, 0, 2)
    before = along_seq(grad[-1], 1)
    behind = along_seq(grad[0], -1)
    tops = shifted(jnp.concatenate([before[None], grad, behind[None]], axis=0))

    def columns(s, earlier, waits):
        pair = (4 - s) % 4
        chip_row = (y + jnp.where(c == 0, -s, s)) % 4
        where = [c, 1 - c, 2 + c, 3 - c, lo * 4 + chip_row, (1 - lo) * 4 + chip_row]
        where = jnp.stack(where).astype(jnp.int32)
        parts = [near[s], near_pair[pair], far[s], far_pair[pair]]
        return back(where, after(tops, *waits), parts, earlier, channels)

    def rows16(value):
        return value.reshape(value.shape[0], 4, 16, value.shape[2])

    feature_grad = columns(0, None, [kept])
    feature_grad = columns(1, feature_grad, [])
    parts = parted(xi, kept, after(taken, feature_grad))
    came, second = over_x(parts[4:])
    feature_grad = columns(2, feature_grad, [came])
    first = rows16(over_y(parts[:4], [feature_grad]))
    _, first = over_x([quarter(first, d) for d in range(4)])
    second = second.reshape(KW, 4, 16, -1)
    second = over_y([second[:, s] for s in range(4)])

    first = (first + other_hi(first)).astype(BF16)
    second = (second + other_hi(second)).astype(BF16)
    feature_grad = columns(3, feature_grad, [second])
    rows = []
    for value in (first, second):
        got = {d: along_x(value, -d) for d in (1, 3, 2)}
        rows += [value, got[1], got[2], got[3]]
    weight_grad = gathered(xi, rows, width)
    return pooled[None], feature_grad[None], weight_grad


def solution(mesh):
    fine = Mesh(mesh.devices.reshape(2, 4, 2, 2, 4), ("zl", "y", "c", "zh", "x"))
    dp, seq = ("zl", "y", "c"), ("zh", "x")
    return jax.shard_map(
        local,
        mesh=fine,
        in_specs=(P(dp, seq, None), P(dp, None), P(dp, seq, None)),
        out_specs=(P(dp, seq, None), P(dp, seq, None), P(dp, None)),
        check_vma=False,
    )
```
